32 devices in a mesh: dp: 4 (over x, core), heads: 8 (over z, y).
Axes of the slice: x: 2, y: 2, z: 4, core: 2. Of those that a mesh axis runs over, the one named last changes fastest.
Arguments:
- latent: bfloat16 [4, 512, 512], P(None, 'dp'), may hold values from -6 to 6
- rope_keys: bfloat16 [4, 512, 64], P(None, 'dp'), may hold values from -6 to 6
- queries: bfloat16 [4, 512, 24576], P(None, 'dp', 'heads'), may hold values from -320 to 320
- grad_out: bfloat16 [4, 512, 16384], P(None, 'dp', 'heads'), may hold values from -2 to 2
- key_value_up_weight: bfloat16 [4, 512, 32768], P('dp', None, 'heads'), may hold values from -0.25 to 0.25
- momentum: bfloat16 [4, 512, 32768], P('dp', None, 'heads'), may hold values from -16 to 16
Outputs:
- new_momentum: bfloat16 [4, 512, 32768], P('dp', None, 'heads')
- layer_update_step: float32 [4, 512, 32768], P('dp', None, 'heads')
The draws below stay inside these ranges and needn't reach their ends.
All inputs are finite; a program needn't handle non-finite values.
Results may differ from the reference program's by a relative error of at most 0.015.
Values may be sent and summed in bfloat16 or wider, within the bound.
A program may use at most 128 MiB of HBM per device.

```python
import math
import jax
import jax.numpy as jnp
from jax import lax

LATENT = 512
HEADS = 128
NOPE = 128
ROPE = 64
VDIM = 128
SEQ = 128
STEPS = 2
LAYERS = 4
TOKENS = 512
COLS = 32768
N_DP = 4


def shared_rope(key):
    base = jax.random.normal(jax.random.fold_in(key, 101), (LAYERS, TOKENS, ROPE), jnp.float32)
    return jnp.clip(base, -6.0, 6.0)


def draw_rope_keys(key, part):
    return shared_rope(key).astype(jnp.bfloat16)


def draw_queries(key, part):
    width = NOPE + ROPE
    shape = (LAYERS, TOKENS, HEADS, width)
    values = jnp.clip(jax.random.normal(jax.random.fold_in(key, 202), shape, jnp.float32), -6.0, 6.0)
    return values.reshape(LAYERS, TOKENS, HEADS * width).astype(jnp.bfloat16)


def head_ramp(key, ratio):
    position = jnp.arange(HEADS, dtype=jnp.float32) / max(HEADS - 1, 1)
    rough = jax.random.uniform(jax.random.fold_in(key, 505), (HEADS,), jnp.float32, 0.7, 1.4)
    return jnp.exp(position * jnp.log(ratio)) * rough


def draw_grad_out(key, part):
    shape = (LAYERS, TOKENS, HEADS, VDIM)
    ramp = 0.03 * head_ramp(key, 10.0)
    base = jnp.clip(jax.random.normal(jax.random.fold_in(key, 606), shape, jnp.float32), -3.0, 3.0)
    values = jnp.clip(base * ramp[None, None, :, None], -2.0, 2.0)
    return values.reshape(LAYERS, TOKENS, HEADS * VDIM).astype(jnp.bfloat16)


def draw_momentum(key, part):
    shape = (LAYERS, LATENT, HEADS, NOPE + VDIM)
    ramp = 0.2 * head_ramp(key, 10.0)
    base = jnp.clip(jax.random.normal(jax.random.fold_in(key, 707), shape, jnp.float32), -3.0, 3.0)
    values = jnp.clip(base * ramp[None, None, :, None], -16.0, 16.0)
    return values.reshape(LAYERS, LATENT, HEADS * (NOPE + VDIM)).astype(jnp.bfloat16)


def block_levels(key, dims, shards, smallest, largest):
    def one(dim, parts):
        heights = jax.random.uniform(jax.random.fold_in(jax.random.fold_in(key, 6), dim), (parts,), jnp.float32, smallest / len(shards), largest / len(shards))
        return jnp.repeat(jnp.exp(heights), dims[dim] // parts).reshape((-1,) + (1,) * (len(dims) - dim - 1))

    factor_of = one(*shards[0])
    for cut in shards[1:]:
        factor_of = factor_of * one(*cut)
    return factor_of


def scatter_about(rng, extent, deviation, bound, pieces=(), kind=jnp.bfloat16):
    array = deviation * jax.random.normal(rng, extent, jnp.float32)
    if pieces:
        array = array * block_levels(rng, extent, pieces, -0.22, 0.18)
    return jnp.clip(array, -bound, bound).astype(kind)


def setup_inputs(seed: int = 0) -> dict:
    key_of = jax.random.split(jax.random.key(seed), 7)
    return {
        "latent": scatter_about(key_of[0], (LAYERS, TOKENS, LATENT), 1.0, 6.0, ((1, 4),)),
        "rope_keys": draw_rope_keys(jax.random.fold_in(key_of[6], 71), 0),
        "queries": draw_queries(jax.random.fold_in(key_of[6], 71), 0),
        "grad_out": draw_grad_out(jax.random.fold_in(key_of[6], 71), 0),
        "key_value_up_weight": scatter_about(key_of[4], (LAYERS, LATENT, COLS), LATENT ** -0.5, 0.25, ((0, 4), (2, 8))),
        "momentum": draw_momentum(jax.random.fold_in(key_of[6], 71), 0),
    }


poly_first = 3.4445
poly_second = -4.775
poly_third = 2.0315
norm_epsilon = 1e-07
decay_rate = 0.95

def sequence_grads(compressed_latent_rows, rotary_position_rows, query_rows, grad_rows, weight_cols):
    rows = compressed_latent_rows.shape[0]
    score_scale = 1.0 / math.sqrt(NOPE + ROPE)
    kv_rows = jnp.dot(compressed_latent_rows, weight_cols, preferred_element_type=jnp.float32).astype(jnp.bfloat16)
    kv_rows = kv_rows.reshape(rows, HEADS, NOPE + VDIM).astype(jnp.float32)
    key_nope = kv_rows[:, :, :NOPE]
    values = kv_rows[:, :, NOPE:]
    query_all = query_rows.reshape(rows, HEADS, NOPE + ROPE).astype(jnp.float32)
    query_nope = query_all[:, :, :NOPE]
    query_rope = query_all[:, :, NOPE:]
    scores = jnp.einsum('shd,thd->hst', query_nope, key_nope)
    scores = scores + jnp.einsum('shd,td->hst', query_rope, rotary_position_rows.astype(jnp.float32))
    scores = scores * score_scale
    places = jnp.arange(rows)
    allowed = places[None, :] <= places[:, None]
    scores = jnp.where(allowed[None], scores, -jnp.inf)
    top_score = lax.optimization_barrier(jnp.max(scores, axis=-1, keepdims=True))
    expd = jnp.exp(scores - top_score)
    probs = expd / lax.optimization_barrier(jnp.sum(expd, axis=-1, keepdims=True))
    probs_low = probs.astype(jnp.bfloat16).astype(jnp.float32)
    grad_heads = grad_rows.reshape(rows, HEADS, VDIM).astype(jnp.float32)
    grad_values = jnp.einsum('hst,shd->thd', probs_low, grad_heads)
    grad_probs = jnp.einsum('shd,thd->hst', grad_heads, values)
    row_delta = lax.optimization_barrier(jnp.sum(probs * grad_probs, axis=-1, keepdims=True))
    grad_scores = (probs * (grad_probs - row_delta) * score_scale).astype(jnp.bfloat16).astype(jnp.float32)
    grad_keys = jnp.einsum('hst,shd->thd', grad_scores, query_nope)
    joined = jnp.concatenate([grad_keys, grad_values], axis=-1).astype(jnp.bfloat16)
    return joined.reshape(rows, HEADS * (NOPE + VDIM))

def orthogonal(source):
    highest = lax.Precision.HIGHEST
    norm_value = jnp.sqrt(jnp.sum(source * source)) + norm_epsilon
    base = jnp.dot(source, source.T, precision=highest) / (norm_value * norm_value)
    identity_matrix = jnp.eye(source.shape[0], dtype=jnp.float32)
    mixer = identity_matrix
    for count_index in range(STEPS):
        inner = jnp.dot(jnp.dot(mixer, base, precision=highest), mixer.T, precision=highest)
        poly = poly_first * identity_matrix + poly_second * inner + poly_third * jnp.dot(inner, inner, precision=highest)
        mixer = jnp.dot(poly, mixer, precision=highest)
    return jnp.dot(mixer, source, precision=highest) / norm_value

def reference(latent, rope_keys, queries, grad_out, key_value_up_weight, momentum):
    update_scale = 0.2 * math.sqrt(max(LATENT, COLS))
    momenta = []
    updates = []
    for layer_index in range(LAYERS):
        total = jnp.zeros((LATENT, COLS), jnp.float32)
        for group_index in range(N_DP):
            low = group_index * SEQ
            compressed_latent_rows = latent[layer_index, low:low + SEQ]
            dkv = sequence_grads(compressed_latent_rows, rope_keys[layer_index, low:low + SEQ], queries[layer_index, low:low + SEQ], grad_out[layer_index, low:low + SEQ], key_value_up_weight[layer_index])
            partial_value = jnp.dot(compressed_latent_rows.T, dkv, preferred_element_type=jnp.float32).astype(jnp.bfloat16)
            partial_value = lax.optimization_barrier(partial_value)
            total = total + partial_value.astype(jnp.float32)
        fresh = (decay_rate * momentum[layer_index].astype(jnp.float32) + total).astype(jnp.bfloat16)
        momenta.append(fresh)
        updates.append(update_scale * orthogonal(fresh.astype(jnp.float32)))
    return (jnp.stack(momenta), jnp.stack(updates))
```

```python
import functools
import math

import jax
import jax.numpy as jnp
from jax import lax
from jax.experimental import pallas as pl
from jax.experimental.pallas import tpu as pltpu
from jax.sharding import PartitionSpec as P

NOPE = 128
ROPE = 64
VDIM = 128
STEPS = 2
PAIR = 2

poly_first = 3.4445
poly_second = -4.775
poly_third = 2.0315
norm_epsilon = 1e-07
decay_rate = 0.95

BF16 = jnp.bfloat16
F32 = jnp.float32
MESH = pl.DeviceIdType.MESH
NT = (((1,), (1,)), ((), ()))


def dot(a, b):
    return jnp.dot(a, b, preferred_element_type=F32)


def dot_nt(a, b):
    return lax.dot_general(a, b, NT, preferred_element_type=F32)


def split(a):
    high = a.astype(BF16)
    return high, (a - high.astype(F32)).astype(BF16)


def dot_wide(a, b):
    ah, al = split(a)
    bh, bl = split(b)
    return dot(ah, bh) + (dot(ah, bl) + dot(al, bh))


def greet(axis, n, me):
    barrier = pltpu.get_barrier_semaphore()
    for k in range(1, n):
        pl.semaphore_signal(
            barrier, inc=1, device_id={axis: lax.rem(me + k, n)}, device_id_type=MESH
        )
    pl.semaphore_wait(barrier, n - 1)


def grads_kernel(
    n, chunks, latent, rope, queries, grad_out, weight, momentum, fresh, gram,
    cbuf, rbuf, qbuf, obuf, wbuf, mbuf, fbuf, small_send, small_recv, big_send, big_recv,
    small_own, big_own, w_sem, m_sem, f_sem,
):
    me = lax.axis_index("dp")
    rows = latent.shape[1]
    width = latent.shape[2]
    qw = PAIR * (NOPE + ROPE)
    ow = PAIR * VDIM
    kw = PAIR * (NOPE + VDIM)
    score_scale = 1.0 / math.sqrt(NOPE + ROPE)

    def columns(c, w):
        return pl.ds(pl.multiple_of(c * w, 128), w)

    def small(k, i):
        to = lax.rem(me + k, n)
        src, dst = ((latent, cbuf), (rope, rbuf))[i]
        return pltpu.make_async_remote_copy(
            src_ref=src.at[to], dst_ref=dst.at[me], send_sem=small_send.at[k - 1, i],
            recv_sem=small_recv.at[k - 1, i], device_id={"dp": to}, device_id_type=MESH,
        )

    def big(k, c, i):
        to = lax.rem(me + k, n)
        src, dst, w = ((queries, qbuf, qw), (grad_out, obuf, ow))[i]
        return pltpu.make_async_remote_copy(
            src_ref=src.at[to, :, columns(c, w)], dst_ref=dst.at[me, :, columns(c, w)],
            send_sem=big_send.at[k - 1, c, i], recv_sem=big_recv.at[k - 1, c, i],
            device_id={"dp": to}, device_id_type=MESH,
        )

    def small_mine(i):
        src, dst = ((latent, cbuf), (rope, rbuf))[i]
        return pltpu.make_async_copy(src.at[me], dst.at[me], small_own.at[i])

    def big_mine(c, i):
        src, dst, w = ((queries, qbuf, qw), (grad_out, obuf, ow))[i]
        return pltpu.make_async_copy(
            src.at[me, :, columns(c, w)], dst.at[me, :, columns(c, w)], big_own.at[c, i]
        )

    def w_copy(c):
        return pltpu.make_async_copy(
            weight.at[:, columns(c, kw)], wbuf.at[:, columns(c, kw)], w_sem.at[c]
        )

    def m_copy(c):
        return pltpu.make_async_copy(
            momentum.at[:, columns(c, kw)], mbuf.at[:, columns(c, kw)], m_sem.at[c]
        )

    def f_copy(c):
        return pltpu.make_async_copy(
            fbuf.at[:, columns(c, kw)], fresh.at[:, columns(c, kw)], f_sem.at[c]
        )

    greet("dp", n, me)
    for i in range(2):
        for k in range(1, n):
            small(k, i).start()
        small_mine(i).start()

    def begin(c, carry):
        for i in range(2):
            for k in range(1, n):
                big(k, c, i).start()
            big_mine(c, i).start()
        w_copy(c).start()
        m_copy(c).start()
        return carry

    lax.fori_loop(0, chunks, begin, 0)
    gram[...] = jnp.zeros_like(gram)
    for i in range(2):
        for k in range(1, n):
            small(k, i).wait_recv()
        small_mine(i).wait()

    earlier = lax.broadcasted_iota(jnp.int32, (rows, rows), 0)
    later = lax.broadcasted_iota(jnp.int32, (rows, rows), 1)
    allowed = earlier <= later

    def work(c, carry):
        for i in range(2):
            for k in range(1, n):
                big(k, c, i).wait_recv()
            big_mine(c, i).wait()
        w_copy(c).wait()
        m_copy(c).wait()
        latents = cbuf[...].reshape(n * rows, width)
        kv = dot(latents, wbuf[:, columns(c, kw)]).astype(BF16)
        parts = []
        for g in range(n):
            here = kv[g * rows:(g + 1) * rows]
            q_all = qbuf[g, :, columns(c, qw)]
            o_all = obuf[g, :, columns(c, ow)]
            for h in range(PAIR):
                key = here[:, h * 256:h * 256 + NOPE]
                value = here[:, h * 256 + NOPE:(h + 1) * 256]
                q_nope = q_all[:, h * 192:h * 192 + NOPE]
                q_rope = q_all[:, h * 192 + NOPE:(h + 1) * 192]
                out_grad = o_all[:, h * VDIM:(h + 1) * VDIM]
                scores = (dot_nt(key, q_nope) + dot_nt(rbuf[g], q_rope)) * score_scale
                scores = jnp.where(allowed, scores, -jnp.inf)
                expd = jnp.exp(scores - jnp.max(scores, axis=0, keepdims=True))
                probs = expd * (1.0 / jnp.sum(expd, axis=0, keepdims=True))
                grad_value = dot(probs.astype(BF16), out_grad)
                grad_probs = dot_nt(value, out_grad)
                delta = jnp.sum(probs * grad_probs, axis=0, keepdims=True)
                grad_scores = (probs * (grad_probs - delta) * score_scale).astype(BF16)
                parts.append(dot(grad_scores, q_nope).astype(BF16))
                parts.append(grad_value.astype(BF16))
        joined = jnp.concatenate(
            [
                jnp.concatenate(parts[g * 2 * PAIR:(g + 1) * 2 * PAIR], axis=1)
                for g in range(n)
            ],
            axis=0,
        )
        grad = lax.dot_general(
            latents, joined, (((0,), (0,)), ((), ())), preferred_element_type=F32
        )
        new = (decay_rate * mbuf[:, columns(c, kw)].astype(F32) + grad).astype(BF16)
        fbuf[:, columns(c, kw)] = new
        gram[...] += dot_nt(new, new)
        f_copy(c).start()
        return carry

    lax.fori_loop(0, chunks, work, 0)

    for i in range(2):
        for k in range(1, n):
            small(k, i).wait_send()

    def finish(c, carry):
        for i in range(2):
            for k in range(1, n):
                big(k, c, i).wait_send()
        f_copy(c).wait()
        return carry

    lax.fori_loop(0, chunks, finish, 0)


def mixer_kernel(
    n, update_scale, gram, high, low, mine, sums, total, first_send, first_recv,
    second_send, second_recv,
):
    me = lax.axis_index("heads")
    size = gram.shape[0]
    block = size // n
    mine[...] = gram[...].astype(BF16).reshape(n, block, size)

    def first(k):
        to = lax.rem(me + k, n)
        return pltpu.make_async_remote_copy(
            src_ref=mine.at[to], dst_ref=sums.at[k - 1], send_sem=first_send.at[k - 1],
            recv_sem=first_recv.at[k - 1], device_id={"heads": to}, device_id_type=MESH,
        )

    def second(k):
        to = lax.rem(me + k, n)
        return pltpu.make_async_remote_copy(
            src_ref=total.at[me], dst_ref=total.at[me], send_sem=second_send.at[k - 1],
            recv_sem=second_recv.at[k - 1], device_id={"heads": to}, device_id_type=MESH,
        )

    greet("heads", n, me)
    for k in range(1, n):
        first(k).start()
    added = mine[me].astype(F32)
    for k in range(1, n):
        first(k).wait_recv()
        added = added + sums[k - 1].astype(F32)
    total[me] = added.astype(BF16)
    for k in range(1, n):
        second(k).start()
    for k in range(1, n):
        second(k).wait_recv()

    raw = total[...].reshape(size, size).astype(F32)
    row = lax.broadcasted_iota(jnp.int32, (size, size), 0)
    col = lax.broadcasted_iota(jnp.int32, (size, size), 1)
    diagonal = row == col
    trace = jnp.sum(
        jnp.sum(jnp.where(diagonal, raw, 0.0), axis=0, keepdims=True), axis=1, keepdims=True
    )
    norm = jnp.sqrt(trace) + norm_epsilon
    base = raw / (norm * norm)
    identity = jnp.where(diagonal, 1.0, 0.0)
    mixer = None
    for step in range(STEPS):
        inner = base if mixer is None else dot_wide(dot_wide(mixer, base), mixer)
        poly = poly_first * identity + poly_second * inner + poly_third * dot_wide(inner, inner)
        mixer = poly if mixer is None else dot_wide(poly, mixer)
    top, rest = split(mixer * (update_scale / norm))
    high[...] = top
    low[...] = rest
    for k in range(1, n):
        first(k).wait_send()
        second(k).wait_send()


def update_kernel(high, low, fresh, kept, update):
    new = fresh[...]
    kept[0] = new
    update[0] = dot(high[...], new) + dot(low[...], new)


def body(n_dp, n_heads, update_scale, latent, rope, queries, grad_out, weight, momentum):
    rows, width = latent.shape[1:]
    heads_here = grad_out.shape[2] // VDIM
    chunks = heads_here // PAIR
    cols = weight.shape[2]
    hbm = pl.BlockSpec(memory_space=pl.ANY)
    vmem = pl.BlockSpec(memory_space=pltpu.VMEM)
    dma = pltpu.SemaphoreType.DMA
    fresh, gram = pl.pallas_call(
        functools.partial(grads_kernel, n_dp, chunks),
        out_shape=(
            jax.ShapeDtypeStruct((width, cols), BF16),
            jax.ShapeDtypeStruct((width, width), F32),
        ),
        in_specs=[hbm] * 6,
        out_specs=(hbm, vmem),
        scratch_shapes=[
            pltpu.VMEM((n_dp, rows, width), BF16),
            pltpu.VMEM((n_dp, rows, ROPE), BF16),
            pltpu.VMEM((n_dp, rows, queries.shape[2]), BF16),
            pltpu.VMEM((n_dp, rows, grad_out.shape[2]), BF16),
            pltpu.VMEM((width, cols), BF16),
            pltpu.VMEM((width, cols), BF16),
            pltpu.VMEM((width, cols), BF16),
            dma((n_dp - 1, 2)),
            dma((n_dp - 1, 2)),
            dma((n_dp - 1, chunks, 2)),
            dma((n_dp - 1, chunks, 2)),
            dma((2,)),
            dma((chunks, 2)),
            dma((chunks,)),
            dma((chunks,)),
            dma((chunks,)),
        ],
        compiler_params=pltpu.CompilerParams(
            collective_id=0, has_side_effects=True, vmem_limit_bytes=48 * 2**20
        ),
        name="grads",
    )(latent, rope, queries, grad_out, weight[0], momentum[0])

    block = width // n_heads
    high, low = pl.pallas_call(
        functools.partial(mixer_kernel, n_heads, update_scale),
        out_shape=(jax.ShapeDtypeStruct((width, width), BF16),) * 2,
        in_specs=[vmem],
        out_specs=(vmem, vmem),
        scratch_shapes=[
            pltpu.VMEM((n_heads, block, width), BF16),
            pltpu.VMEM((n_heads - 1, block, width), BF16),
            pltpu.VMEM((n_heads, block, width), BF16),
            dma((n_heads - 1,)),
            dma((n_heads - 1,)),
            dma((n_heads - 1,)),
            dma((n_heads - 1,)),
        ],
        compiler_params=pltpu.CompilerParams(
            collective_id=1, has_side_effects=True, vmem_limit_bytes=48 * 2**20
        ),
        name="mixer",
    )(gram)

    tile = 512
    return pl.pallas_call(
        update_kernel,
        grid=(cols // tile,),
        out_shape=(
            jax.ShapeDtypeStruct((1, width, cols), BF16),
            jax.ShapeDtypeStruct((1, width, cols), F32),
        ),
        in_specs=[
            pl.BlockSpec((width, width), lambda j: (0, 0)),
            pl.BlockSpec((width, width), lambda j: (0, 0)),
            pl.BlockSpec((width, tile), lambda j: (0, j)),
        ],
        out_specs=(
            pl.BlockSpec((1, width, tile), lambda j: (0, 0, j)),
            pl.BlockSpec((1, width, tile), lambda j: (0, 0, j)),
        ),
        compiler_params=pltpu.CompilerParams(vmem_limit_bytes=32 * 2**20),
        name="update",
    )(high, low, fresh)


def solution(mesh):
    n_dp = mesh.shape["dp"]
    n_heads = mesh.shape["heads"]
    placed = (
        P(None, "dp", None),
        P(None, "dp", None),
        P(None, "dp", "heads"),
        P(None, "dp", "heads"),
        P("dp", None, "heads"),
        P("dp", None, "heads"),
    )

    def whole(latent, rope_keys, queries, grad_out, key_value_up_weight, momentum):
        _, width, cols = key_value_up_weight.shape
        update_scale = 0.2 * math.sqrt(max(width, cols))
        return jax.shard_map(
            functools.partial(body, n_dp, n_heads, update_scale),
            mesh=mesh,
            in_specs=placed,
            out_specs=(P("dp", None, "heads"), P("dp", None, "heads")),
            check_vma=False,
        )(latent, rope_keys, queries, grad_out, key_value_up_weight, momentum)

    return whole
```

```python
import functools
import math

import jax
import jax.numpy as jnp
from jax import lax
from jax.experimental import pallas as pl
from jax.experimental.pallas import tpu as pltpu
from jax.sharding import PartitionSpec as P

NOPE = 128
ROPE = 64
VDIM = 128
STEPS = 2
PAIR = 2
TILE = 128

poly_first = 3.4445
poly_second = -4.775
poly_third = 2.0315
norm_epsilon = 1e-07
decay_rate = 0.95

BF16 = jnp.bfloat16
F32 = jnp.float32
MESH = pl.DeviceIdType.MESH
NT = (((1,), (1,)), ((), ()))


def dot(a, b):
    return jnp.dot(a, b, preferred_element_type=F32)


def dot_nt(a, b):
    return lax.dot_general(a, b, NT, preferred_element_type=F32)


def split(a):
    high = a.astype(BF16)
    return high, (a - high.astype(F32)).astype(BF16)


def dot_wide(a, b):
    ah, al = split(a)
    bh, bl = split(b)
    return dot(ah, bh) + (dot(ah, bl) + dot(al, bh))


def upper(size):
    blocks = size // TILE
    return [(i, j) for i in range(blocks) for j in range(i, blocks)]


def greet(axis, n, me):
    barrier = pltpu.get_barrier_semaphore()
    for k in range(1, n):
        pl.semaphore_signal(
            barrier, inc=1, device_id={axis: lax.rem(me + k, n)}, device_id_type=MESH
        )
    pl.semaphore_wait(barrier, n - 1)


def grads_kernel(
    n, chunks, latent, rope, queries, grad_out, weight, momentum, fresh, packed,
    cbuf, rbuf, turned, qbuf, obuf, wbuf, mbuf, fbuf, whole, small_send, small_recv, big_send, big_recv,
    small_own, big_own, w_sem, m_sem, f_sem,
):
    me = lax.axis_index("dp")
    rows = latent.shape[1]
    width = latent.shape[2]
    qw = PAIR * (NOPE + ROPE)
    ow = PAIR * VDIM
    kw = PAIR * (NOPE + VDIM)
    score_scale = 1.0 / math.sqrt(NOPE + ROPE)

    def columns(c, w):
        return pl.ds(pl.multiple_of(c * w, 128), w)

    def small(k, i):
        to = lax.rem(me + k, n)
        src, dst = ((latent, cbuf), (rope, rbuf))[i]
        return pltpu.make_async_remote_copy(
            src_ref=src.at[to], dst_ref=dst.at[me], send_sem=small_send.at[k - 1, i],
            recv_sem=small_recv.at[k - 1, i], device_id={"dp": to}, device_id_type=MESH,
        )

    def big(k, c, i):
        to = lax.rem(me + k, n)
        src, dst, w = ((queries, qbuf, qw), (grad_out, obuf, ow))[i]
        return pltpu.make_async_remote_copy(
            src_ref=src.at[to, :, columns(c, w)], dst_ref=dst.at[me, :, columns(c, w)],
            send_sem=big_send.at[k - 1, c, i], recv_sem=big_recv.at[k - 1, c, i],
            device_id={"dp": to}, device_id_type=MESH,
        )

    def small_mine(i):
        src, dst = ((latent, cbuf), (rope, rbuf))[i]
        return pltpu.make_async_copy(src.at[me], dst.at[me], small_own.at[i])

    def big_mine(c, i):
        src, dst, w = ((queries, qbuf, qw), (grad_out, obuf, ow))[i]
        return pltpu.make_async_copy(
            src.at[me, :, columns(c, w)], dst.at[me, :, columns(c, w)], big_own.at[c, i]
        )

    def w_copy(c):
        return pltpu.make_async_copy(
            weight.at[:, columns(c, kw)], wbuf.at[:, columns(c, kw)], w_sem.at[c]
        )

    def m_copy(c):
        return pltpu.make_async_copy(
            momentum.at[:, columns(c, kw)], mbuf.at[:, columns(c, kw)], m_sem.at[c]
        )

    def f_copy(c):
        return pltpu.make_async_copy(
            fbuf.at[:, columns(c, kw)], fresh.at[:, columns(c, kw)], f_sem.at[c]
        )

    greet("dp", n, me)
    for i in range(2):
        for k in range(1, n):
            small(k, i).start()
        small_mine(i).start()

    def begin(c, carry):
        for i in range(2):
            for k in range(1, n):
                big(k, c, i).start()
            big_mine(c, i).start()
        w_copy(c).start()
        m_copy(c).start()
        return carry

    lax.fori_loop(0, chunks, begin, 0)
    whole[...] = jnp.zeros_like(whole)
    for i in range(2):
        for k in range(1, n):
            small(k, i).wait_recv()
        small_mine(i).wait()

    for g in range(n):
        turned[g] = rbuf[g].astype(F32).T.astype(BF16)

    earlier = lax.broadcasted_iota(jnp.int32, (rows, rows), 0)
    later = lax.broadcasted_iota(jnp.int32, (rows, rows), 1)
    allowed = earlier <= later

    def work(c, carry):
        for i in range(2):
            for k in range(1, n):
                big(k, c, i).wait_recv()
            big_mine(c, i).wait()
        w_copy(c).wait()
        m_copy(c).wait()
        latents = cbuf[...].reshape(n * rows, width)
        kv = dot(latents, wbuf[:, columns(c, kw)]).astype(BF16)
        parts = []
        for g in range(n):
            here = kv[g * rows:(g + 1) * rows]
            q_all = qbuf[g, :, columns(c, qw)]
            o_all = obuf[g, :, columns(c, ow)]
            for h in range(PAIR):
                key = here[:, h * 256:h * 256 + NOPE]
                value = here[:, h * 256 + NOPE:(h + 1) * 256]
                q_nope = q_all[:, h * 192:h * 192 + NOPE]
                q_rope = q_all[:, h * 192 + NOPE:(h + 1) * 192]
                out_grad = o_all[:, h * VDIM:(h + 1) * VDIM]
                scores = (dot_nt(key, q_nope) + dot_nt(turned[g], q_rope)) * score_scale
                scores = jnp.where(allowed, scores, -jnp.inf)
                expd = jnp.exp(scores - jnp.max(scores, axis=0, keepdims=True))
                probs = expd * (1.0 / jnp.sum(expd, axis=0, keepdims=True))
                grad_value = dot(probs.astype(BF16), out_grad)
                grad_probs = dot_nt(value, out_grad)
                delta = jnp.sum(probs * grad_probs, axis=0, keepdims=True)
                grad_scores = (probs * (grad_probs - delta) * score_scale).astype(BF16)
                parts.append(dot(grad_scores, q_nope).astype(BF16))
                parts.append(grad_value.astype(BF16))
        joined = jnp.concatenate(
            [
                jnp.concatenate(parts[g * 2 * PAIR:(g + 1) * 2 * PAIR], axis=1)
                for g in range(n)
            ],
            axis=0,
        )
        grad = lax.dot_general(
            latents, joined, (((0,), (0,)), ((), ())), preferred_element_type=F32
        )
        new = (decay_rate * mbuf[:, columns(c, kw)].astype(F32) + grad).astype(BF16)
        fbuf[:, columns(c, kw)] = new
        whole[...] += dot_nt(new, new)
        f_copy(c).start()
        return carry

    lax.fori_loop(0, chunks, work, 0)
    for p, (i, j) in enumerate(upper(width)):
        packed[pl.ds(p * TILE, TILE), :] = whole[
            pl.ds(i * TILE, TILE), pl.ds(j * TILE, TILE)
        ].astype(BF16)

    for i in range(2):
        for k in range(1, n):
            small(k, i).wait_send()

    def finish(c, carry):
        for i in range(2):
            for k in range(1, n):
                big(k, c, i).wait_send()
        f_copy(c).wait()
        return carry

    lax.fori_loop(0, chunks, finish, 0)


def mixer_kernel(
    n, update_scale, mine, high, low, sums, total, full, first_send, first_recv,
    second_send, second_recv,
):
    me = lax.axis_index("heads")
    size = high.shape[0]
    pairs = upper(size)
    block = len(pairs) * TILE // n

    def part(k):
        return pl.ds(pl.multiple_of(k * block, 16), block)

    def first(k):
        to = lax.rem(me + k, n)
        return pltpu.make_async_remote_copy(
            src_ref=mine.at[part(to)], dst_ref=sums.at[k - 1], send_sem=first_send.at[k - 1],
            recv_sem=first_recv.at[k - 1], device_id={"heads": to}, device_id_type=MESH,
        )

    def second(k):
        to = lax.rem(me + k, n)
        return pltpu.make_async_remote_copy(
            src_ref=total.at[part(me)], dst_ref=total.at[part(me)], send_sem=second_send.at[k - 1],
            recv_sem=second_recv.at[k - 1], device_id={"heads": to}, device_id_type=MESH,
        )

    greet("heads", n, me)
    for k in range(1, n):
        first(k).start()
    added = mine[part(me), :].astype(F32)
    for k in range(1, n):
        first(k).wait_recv()
        added = added + sums[k - 1].astype(F32)
    total[part(me), :] = added.astype(BF16)
    for k in range(1, n):
        second(k).start()
    for k in range(1, n):
        second(k).wait_recv()

    for p, (i, j) in enumerate(pairs):
        here = total[pl.ds(p * TILE, TILE), :].astype(F32)
        full[pl.ds(i * TILE, TILE), pl.ds(j * TILE, TILE)] = here
        if i != j:
            full[pl.ds(j * TILE, TILE), pl.ds(i * TILE, TILE)] = here.T
    raw = full[...]
    row = lax.broadcasted_iota(jnp.int32, (size, size), 0)
    col = lax.broadcasted_iota(jnp.int32, (size, size), 1)
    diagonal = row == col
    trace = jnp.sum(
        jnp.sum(jnp.where(diagonal, raw, 0.0), axis=0, keepdims=True), axis=1, keepdims=True
    )
    norm = jnp.sqrt(trace) + norm_epsilon
    base = raw / (norm * norm)
    identity = jnp.where(diagonal, 1.0, 0.0)
    mixer = None
    for step in range(STEPS):
        inner = base if mixer is None else dot_wide(dot_wide(mixer, base), mixer)
        poly = poly_first * identity + poly_second * inner + poly_third * dot_wide(inner, inner)
        mixer = poly if mixer is None else dot_wide(poly, mixer)
    top, rest = split(mixer * (update_scale / norm))
    high[...] = top
    low[...] = rest
    for k in range(1, n):
        first(k).wait_send()
        second(k).wait_send()


def update_kernel(high, low, fresh, kept, update):
    new = fresh[...]
    kept[0] = new
    update[0] = dot(high[...], new) + dot(low[...], new)


def body(n_dp, n_heads, update_scale, latent, rope, queries, grad_out, weight, momentum):
    rows, width = latent.shape[1:]
    heads_here = grad_out.shape[2] // VDIM
    chunks = heads_here // PAIR
    packed = len(upper(width)) * TILE
    cols = weight.shape[2]
    hbm = pl.BlockSpec(memory_space=pltpu.HBM)
    vmem = pl.BlockSpec(memory_space=pltpu.VMEM)
    dma = pltpu.SemaphoreType.DMA
    fresh, gram = pl.pallas_call(
        functools.partial(grads_kernel, n_dp, chunks),
        out_shape=(
            jax.ShapeDtypeStruct((width, cols), BF16),
            jax.ShapeDtypeStruct((packed, TILE), BF16),
        ),
        in_specs=[hbm] * 6,
        out_specs=(hbm, vmem),
        scratch_shapes=[
            pltpu.VMEM((n_dp, rows, width), BF16),
            pltpu.VMEM((n_dp, ROPE, rows), BF16),
            pltpu.VMEM((n_dp, rows, ROPE), BF16),
            pltpu.VMEM((n_dp, rows, queries.shape[2]), BF16),
            pltpu.VMEM((n_dp, rows, grad_out.shape[2]), BF16),
            pltpu.VMEM((width, cols), BF16),
            pltpu.VMEM((width, cols), BF16),
            pltpu.VMEM((width, cols), BF16),
            pltpu.VMEM((width, width), F32),
            dma((n_dp - 1, 2)),
            dma((n_dp - 1, 2)),
            dma((n_dp - 1, chunks, 2)),
            dma((n_dp - 1, chunks, 2)),
            dma((2,)),
            dma((chunks, 2)),
            dma((chunks,)),
            dma((chunks,)),
            dma((chunks,)),
        ],
        compiler_params=pltpu.CompilerParams(
            collective_id=0, has_side_effects=True, vmem_limit_bytes=56 * 2**20
        ),
        name="grads",
    )(latent, jnp.swapaxes(rope, 1, 2), queries, grad_out, weight[0], momentum[0])

    block = packed // n_heads
    high, low = pl.pallas_call(
        functools.partial(mixer_kernel, n_heads, update_scale),
        out_shape=(jax.ShapeDtypeStruct((width, width), BF16),) * 2,
        in_specs=[vmem],
        out_specs=(vmem, vmem),
        scratch_shapes=[
            pltpu.VMEM((n_heads - 1, block, TILE), BF16),
            pltpu.VMEM((packed, TILE), BF16),
            pltpu.VMEM((width, width), F32),
            dma((n_heads - 1,)),
            dma((n_heads - 1,)),
            dma((n_heads - 1,)),
            dma((n_heads - 1,)),
        ],
        compiler_params=pltpu.CompilerParams(
            collective_id=1, has_side_effects=True, vmem_limit_bytes=24 * 2**20
        ),
        name="mixer",
    )(gram)

    tile = 512
    return pl.pallas_call(
        update_kernel,
        grid=(cols // tile,),
        out_shape=(
            jax.ShapeDtypeStruct((1, width, cols), BF16),
            jax.ShapeDtypeStruct((1, width, cols), F32),
        ),
        in_specs=[
            pl.BlockSpec((width, width), lambda j: (0, 0)),
            pl.BlockSpec((width, width), lambda j: (0, 0)),
            pl.BlockSpec((width, tile), lambda j: (0, j)),
        ],
        out_specs=(
            pl.BlockSpec((1, width, tile), lambda j: (0, 0, j)),
            pl.BlockSpec((1, width, tile), lambda j: (0, 0, j)),
        ),
        compiler_params=pltpu.CompilerParams(vmem_limit_bytes=52 * 2**20),
        name="update",
    )(high, low, fresh)


def solution(mesh):
    n_dp = mesh.shape["dp"]
    n_heads = mesh.shape["heads"]
    placed = (
        P(None, "dp", None),
        P(None, "dp", None),
        P(None, "dp", "heads"),
        P(None, "dp", "heads"),
        P("dp", None, "heads"),
        P("dp", None, "heads"),
    )

    def whole(latent, rope_keys, queries, grad_out, key_value_up_weight, momentum):
        _, width, cols = key_value_up_weight.shape
        update_scale = 0.2 * math.sqrt(max(width, cols))
        return jax.shard_map(
            functools.partial(body, n_dp, n_heads, update_scale),
            mesh=mesh,
            in_specs=placed,
            out_specs=(P("dp", None, "heads"), P("dp", None, "heads")),
            check_vma=False,
        )(latent, rope_keys, queries, grad_out, key_value_up_weight, momentum)

    return whole
```
